32 devices in a mesh: dp: 8 (over y, x, core), mp: 4 (over z).
Axes of the slice: x: 2, y: 2, z: 4, core: 2. Of those that a mesh axis runs over, the one named last changes fastest.
Arguments:
- clean_image: bfloat16 [4, 588, 128], P('mp'), may hold values from -6 to 6
- noise_draw: bfloat16 [4, 8, 588, 128], P('mp', 'dp'), may hold values from -6 to 6
- embed_weight: bfloat16 [588, 6144], P(None, 'dp'), may hold values from -0.25 to 0.25
- position_table: bfloat16 [128, 6144], replicated, may hold values from -3 to 3
- norm_gain: float32 [6144], replicated, may hold values from 0.1 to 1.9
- qkv_weight: bfloat16 [6144, 3, 3072], P(None, None, 'mp'), may hold values from -0.078125 to 0.078125
- query_gain: float32 [128], replicated, may hold values from 0.1 to 1.9
- key_gain: float32 [128], replicated, may hold values from 0.1 to 1.9
- out_weight: bfloat16 [3072, 6144], P('mp'), may hold values from -0.375 to 0.375
Outputs:
- features: bfloat16 [128, 8, 4, 6144], P(None, 'dp', 'mp')
- smoothed: float32 [128, 4, 6144], P(None, 'mp', 'dp')
The draws below stay inside these ranges and needn't reach their ends.
All inputs are finite; a program needn't handle non-finite values.
Results may differ from the reference program's by a relative error of at most 0.017.
Values may be sent and summed in bfloat16 or wider, within the bound.
A program may use at most 128 MiB of HBM per device.

```python
import jax
import jax.numpy as jnp
from jax import lax

D = 6144
HEAD_DIM = 128
PIX = 588
HEADS = 24
PATCHES = 128
IMAGES = 4
COPIES = 8
N_MP = 4


def shard_levels(stream_key, dims, split, least, largest):
    def one(position, blocks):
        draws = jax.random.uniform(jax.random.fold_in(jax.random.fold_in(stream_key, 6), position), (blocks,), jnp.float32, least / len(split), largest / len(split))
        return jnp.repeat(jnp.exp(draws), dims[position] // blocks).reshape((-1,) + (1,) * (len(dims) - position - 1))

    level = one(*split[0])
    for cut in split[1:]:
        level = level * one(*cut)
    return level


def scatter_about(key, dims, scale, limit, shards=(), dtype=jnp.bfloat16):
    drawn = scale * jax.random.normal(key, dims, jnp.float32)
    if shards:
        drawn = drawn * shard_levels(key, dims, shards, -0.22, 0.18)
    return jnp.clip(drawn, -limit, limit).astype(dtype)


def setup_inputs(seed: int = 0) -> dict:
    key_list = jax.random.split(jax.random.key(seed), 10)
    return {
        "clean_image": scatter_about(key_list[0], (IMAGES, PIX, PATCHES), 1.0, 6.0, ((0, 4),)),
        "noise_draw": scatter_about(key_list[1], (IMAGES, COPIES, PIX, PATCHES), 1.0, 6.0, ((0, 4), (1, 8))),
        "embed_weight": scatter_about(key_list[2], (PIX, D), PIX ** -0.5, 0.25, ((1, 8),)),
        "position_table": scatter_about(key_list[3], (PATCHES, D), 0.5, 3.0),
        "norm_gain": jnp.clip(1.0 + 0.18 * jax.random.normal(key_list[4], (D,), jnp.float32), 0.1, 1.9),
        "qkv_weight": scatter_about(key_list[5], (D, 3, HEADS * HEAD_DIM), D ** -0.5, 0.078125, ((2, 4),)),
        "query_gain": jnp.clip(1.0 + 0.18 * jax.random.normal(key_list[6], (HEAD_DIM,), jnp.float32), 0.1, 1.9),
        "key_gain": jnp.clip(1.0 + 0.18 * jax.random.normal(key_list[7], (HEAD_DIM,), jnp.float32), 0.1, 1.9),
        "out_weight": scatter_about(key_list[8], (HEADS * HEAD_DIM, D), (2 * HEAD_DIM) ** -0.5, 0.375, ((0, 4),)),
    }


epsilon = 1e-06

def layer_norm(values, gain_vec):
    average = lax.optimization_barrier(jnp.mean(values, axis=-1, keepdims=True))
    centred = values - average
    variance = lax.optimization_barrier(jnp.mean(centred * centred, axis=-1, keepdims=True))
    return centred * lax.rsqrt(variance + epsilon) * gain_vec

def reference(clean_image, noise_draw, embed_weight, position_table, norm_gain, qkv_weight, query_gain, key_gain, out_weight):
    highest = lax.Precision.HIGHEST
    num_images = clean_image.shape[0]
    num_patches = clean_image.shape[2]
    num_copies = noise_draw.shape[1]
    width = embed_weight.shape[1]
    group = HEADS * HEAD_DIM // N_MP
    position_f = position_table.astype(jnp.float32)
    copies_first = jnp.moveaxis(noise_draw, 1, 0)

    def one_copy(carry, copy_noise):
        noisy_img = (clean_image.astype(jnp.float32) + 0.5 * copy_noise.astype(jnp.float32)).astype(jnp.bfloat16)
        embedded = jnp.einsum('ikp,kd->pid', noisy_img.astype(jnp.float32), embed_weight.astype(jnp.float32), precision=highest) + position_f[:, None, :]
        normed = layer_norm(embedded, norm_gain).astype(jnp.bfloat16)
        projected = jnp.einsum('pid,dtc->pitc', normed.astype(jnp.float32), qkv_weight.astype(jnp.float32), precision=highest)
        query = projected[:, :, 0].reshape(num_patches, num_images, HEADS, HEAD_DIM)
        key_vec = projected[:, :, 1].reshape(num_patches, num_images, HEADS, HEAD_DIM)
        value = projected[:, :, 2].reshape(num_patches, num_images, HEADS, HEAD_DIM).astype(jnp.bfloat16)
        query = layer_norm(query, query_gain).astype(jnp.bfloat16)
        key_vec = layer_norm(key_vec, key_gain).astype(jnp.bfloat16)
        scores = jnp.einsum('pihe,sihe->ihps', query.astype(jnp.float32), key_vec.astype(jnp.float32), precision=highest) * HEAD_DIM ** (-0.5)
        exp_scores = jnp.exp(scores)
        probs = (exp_scores / lax.optimization_barrier(jnp.sum(exp_scores, axis=-1, keepdims=True))).astype(jnp.bfloat16)
        head_out = jnp.einsum('ihps,sihe->pihe', probs.astype(jnp.float32), value.astype(jnp.float32), precision=highest)
        head_out = head_out.astype(jnp.bfloat16).reshape(num_patches, num_images, HEADS * HEAD_DIM)
        attention = jnp.zeros((num_patches, num_images, width), jnp.float32)
        for group_index in range(N_MP):
            lower = group_index * group
            partial_sum = jnp.einsum('pic,cd->pid', head_out[:, :, lower:lower + group].astype(jnp.float32), out_weight[lower:lower + group].astype(jnp.float32), precision=highest)
            partial_sum = lax.optimization_barrier(partial_sum.astype(jnp.bfloat16)).astype(jnp.float32)
            attention = attention + partial_sum
        output = embedded + attention
        carry = carry + output * (1.0 / num_copies)
        return (carry, output.astype(jnp.bfloat16))
    start_sum = jnp.zeros((num_patches, num_images, width), jnp.float32)
    smoothed, stacked = lax.scan(one_copy, start_sum, copies_first)
    features = jnp.moveaxis(stacked, 0, 1)
    return (features, smoothed)
```

```python
import functools

import jax
import jax.numpy as jnp
from jax import lax
from jax.experimental import pallas as pl
from jax.experimental.pallas import tpu as pltpu
from jax.sharding import PartitionSpec as P

HEAD_DIM = 128
MESH = pl.DeviceIdType.MESH
EPSILON = 1e-06


def round_up(value, step):
    return (value + step - 1) // step * step


def remote(src, dst, send_sem, recv_sem, axis, target):
    return pltpu.make_async_remote_copy(
        src_ref=src,
        dst_ref=dst,
        send_sem=send_sem,
        recv_sem=recv_sem,
        device_id={axis: target},
        device_id_type=MESH,
    )


def greet(sizes):
    barrier = pltpu.get_barrier_semaphore()
    total = 0
    for axis, size in sizes:
        me = lax.axis_index(axis)
        for step in range(1, size):
            pl.semaphore_signal(
                barrier,
                inc=1,
                device_id={axis: lax.rem(me + step, size)},
                device_id_type=MESH,
            )
        total += size - 1
    pl.semaphore_wait(barrier, total)


class Gather:
    def __init__(self, size, own, slot, halves, send_sem, recv_sem, half_sem):
        self.size = size
        self.me = lax.axis_index("dp")
        self.core = lax.rem(self.me, 2)
        self.chip = self.me // 2
        self.chips = size // 2
        self.own, self.slot, self.halves = own, slot, halves
        self.send_sem, self.recv_sem, self.half_sem = send_sem, recv_sem, half_sem
        self.sent = []
        self.relay = self.chips == 4
        self.sibling = self.chip * 2 + 1 - self.core
        if self.relay:
            x = self.chip + 1 - 2 * lax.rem(self.chip, 2)
            y = lax.rem(self.chip + 2, 4)
            d = lax.rem(x + 2, 4)
            self.order = [x, y, d]
        else:
            self.order = [lax.rem(self.chip + j, self.chips) for j in range(1, self.chips)]

    def push(self, src, dst, recv, target):
        copy = remote(src, dst, self.send_sem.at[len(self.sent)], recv, "dp", target)
        copy.start()
        self.sent.append(copy)

    def start(self):
        me = self.me
        for chip in self.order[: 2 if self.relay else None]:
            self.push(self.own, self.slot(me), self.recv_sem.at[me], chip * 2 + self.core)
        self.push(self.own, self.slot(me), self.recv_sem.at[me], self.sibling)

    def wait_slot(self, source):
        there = self.slot(source)
        remote(there, there, self.send_sem.at[0], self.recv_sem.at[source], "dp", self.sibling).wait_recv()

    def to_sibling(self, source):
        there = self.slot(source)
        self.push(there, there, self.recv_sem.at[source], self.sibling)

    def arrive(self, step):
        source = self.order[step] * 2 + self.core
        if self.relay and step == 2:
            for half in range(2):
                part = self.halves(source, half)
                remote(part, part, self.send_sem.at[0], self.half_sem.at[half], "dp", self.sibling).wait_recv()
        else:
            self.wait_slot(source)
            if self.relay:
                part = self.halves(source, step)
                other = self.order[1 - step] * 2 + self.core
                self.push(part, part, self.half_sem.at[step], other)
        self.to_sibling(source)
        return source

    def arrive_sibling(self, step):
        source = self.order[step] * 2 + 1 - self.core
        self.wait_slot(source)
        return source

    def finish(self):
        for copy in self.sent:
            copy.wait_send()


def sends(size):
    chips = size // 2
    return (chips - 1) + 1 + (chips - 1) + 2


def heads_kernel(
    nd, nm, noisy_ref, embed_ref, position_ref, gain_ref, qkv_ref, qgain_ref, kgain_ref, out_ref,
    pixels, blocks, embedded, normed, weights, projected, outgoing, arrived,
    z_send, z_recv, w_send, w_recv, w_half, h_send, h_recv, load_sem,
):
    here = lax.axis_index("mp")
    patches = position_ref.shape[0]
    width = embed_ref.shape[1]
    rows, rows_full = embed_ref.shape[0], blocks.shape[1]
    total = nm * patches
    pairs, chunk = outgoing.shape[0], outgoing.shape[3]
    heads = chunk // HEAD_DIM

    def load(kind, pair):
        return pltpu.make_async_copy(
            qkv_ref.at[kind, :, pl.ds(pl.multiple_of(pair * chunk, HEAD_DIM), chunk)],
            weights.at[kind],
            load_sem.at[kind],
        )

    for kind in range(3):
        load(kind, 0).start()
    if rows_full > rows:
        blocks[:, rows:, :] = jnp.zeros((nd, rows_full - rows, width), blocks.dtype)
    greet((("dp", nd), ("mp", nm)))

    gather = Gather(
        nd,
        embed_ref,
        lambda s: blocks.at[s, pl.ds(0, rows)],
        lambda s, half: blocks.at[s, pl.ds(0, rows), pl.ds(half * (width // 2), width // 2)],
        w_send, w_recv, w_half,
    )
    pixel_copies = []
    for step in range(1, nm):
        copy = remote(
            noisy_ref, pixels.at[here], z_send.at[step - 1], z_recv.at[here], "mp",
            lax.rem(here + step, nm),
        )
        copy.start()
        pixel_copies.append(copy)
    gather.start()
    pixels[here] = noisy_ref[...]
    blocks[gather.me, :rows, :] = embed_ref[...]
    for step in range(1, nm):
        source = lax.rem(here + step, nm)
        remote(
            noisy_ref, pixels.at[source], z_send.at[0], z_recv.at[source], "mp", source
        ).wait_recv()

    part = 256 if width % 256 == 0 else 128

    def embed(source):
        @pl.loop(0, width // part)
        def _(n):
            cols = pl.ds(pl.multiple_of(n * part, part), part)
            product = jnp.dot(
                pixels[...].reshape(total, rows_full),
                blocks[source, :, cols],
                preferred_element_type=jnp.float32,
            )
            place = position_ref[:, pl.ds(pl.multiple_of(source * width + n * part, part), part)]
            product = product.reshape(nm, patches, part) + place.astype(jnp.float32)[None]
            embedded[source, :, cols] = product.reshape(total, part)

    embed(gather.me)
    steps = len(gather.order)
    gather.wait_slot(gather.sibling)
    embed(gather.sibling)
    if gather.relay:
        near = [gather.arrive(0), gather.arrive(1)]
        for source in near:
            embed(source)
        for step in range(2):
            embed(gather.arrive_sibling(step))
        embed(gather.arrive(2))
        embed(gather.arrive_sibling(2))
    else:
        for step in range(steps):
            embed(gather.arrive(step))
        for step in range(steps):
            embed(gather.arrive_sibling(step))

    band = 16
    features = nd * width

    @pl.loop(0, total // band)
    def _(r):
        at = pl.ds(pl.multiple_of(r * band, band), band)
        values = embedded[:, at, :]
        mean = jnp.sum(jnp.sum(values, axis=0), axis=-1, keepdims=True) * (1.0 / features)
        centred = embedded[:, at, :] - mean[None]
        square = jnp.sum(jnp.sum(centred * centred, axis=0), axis=-1, keepdims=True)
        scale = lax.rsqrt(square * (1.0 / features) + EPSILON)
        normed[:, at, :] = (
            (embedded[:, at, :] - mean[None]) * scale[None] * gain_ref[...]
        ).astype(normed.dtype)

    def head_norm(values, gain):
        mean = jnp.mean(values, axis=-1, keepdims=True)
        centred = values - mean
        variance = jnp.mean(centred * centred, axis=-1, keepdims=True)
        return (centred * lax.rsqrt(variance + EPSILON) * gain[...]).astype(jnp.bfloat16)

    def exchange(pair, step):
        target = lax.rem(here + step, nm)
        return remote(
            outgoing.at[pair, target], arrived.at[here, pair],
            h_send.at[pair, step - 1], h_recv.at[pair, here], "mp", target,
        )

    @pl.loop(0, pairs)
    def _(pair):
        for kind in range(3):
            load(kind, pair).wait()
            for s in range(nd):
                product = jnp.dot(
                    normed[s], weights[kind, s * width : (s + 1) * width, :],
                    preferred_element_type=jnp.float32,
                )
                if s == 0:
                    projected[kind] = product
                else:
                    projected[kind] += product

            @pl.when(pair + 1 < pairs)
            def _():
                load(kind, pair + 1).start()

        @pl.loop(0, nm)
        def _(image):
            at = pl.ds(pl.multiple_of(image * patches, patches), patches)
            for head in range(heads):
                cols = slice(head * HEAD_DIM, (head + 1) * HEAD_DIM)
                query = head_norm(projected[0, at, cols], qgain_ref)
                key = head_norm(projected[1, at, cols], kgain_ref)
                value = projected[2, at, cols].astype(jnp.bfloat16)
                scores = lax.dot_general(
                    query, key, (((1,), (1,)), ((), ())), preferred_element_type=jnp.float32
                ) * HEAD_DIM ** (-0.5)
                powers = jnp.exp(scores)
                probs = (powers / jnp.sum(powers, axis=-1, keepdims=True)).astype(jnp.bfloat16)
                result = jnp.dot(probs, value, preferred_element_type=jnp.float32)
                outgoing[pair, image, :, cols] = result.astype(jnp.bfloat16)

        for step in range(1, nm):
            exchange(pair, step).start()
        arrived[here, pair] = outgoing[pair, here]

    for copy in pixel_copies:
        copy.wait_send()
    gather.finish()
    for pair in range(pairs):
        for step in range(1, nm):
            exchange(pair, step).wait_send()
            source = lax.rem(here + step, nm)
            remote(
                outgoing.at[pair, source], arrived.at[source, pair],
                h_send.at[pair, step - 1], h_recv.at[pair, source], "mp", source,
            ).wait_recv()
    out_ref[...] = arrived[...]


def output_kernel(
    nd, heads_ref, noisy_ref, embed_ref, position_ref, out_weight_ref, features_ref, smoothed_ref,
    held, residual, outgoing, incoming, g_send, g_recv, g_half, f_send, f_recv,
):
    me = lax.axis_index("dp")
    nm, pairs, patches, chunk = heads_ref.shape
    width = embed_ref.shape[1]
    rows = embed_ref.shape[0]
    greet((("dp", nd),))
    gather = Gather(
        nd,
        heads_ref,
        lambda s: held.at[s],
        lambda s, half: held.at[s, pl.ds(half * (nm // 2), nm // 2)],
        g_send, g_recv, g_half,
    )
    gather.start()
    held[me] = heads_ref[...]
    place = position_ref[...].astype(jnp.float32)

    @pl.loop(0, nd)
    def _(c):
        residual[c] = (
            jnp.dot(noisy_ref[c], embed_ref[...], preferred_element_type=jnp.float32) + place
        )

    smoothed_ref[...] = jnp.zeros_like(smoothed_ref)
    part = 256 if width % 256 == 0 else 128
    both = 2 * patches

    def give(copy):
        return remote(
            outgoing.at[copy], incoming.at[me], f_send.at[copy], f_recv.at[me], "dp", copy
        )

    def project(chip):
        first = chip * 2

        @pl.loop(0, width // part)
        def _(n):
            cols = pl.ds(pl.multiple_of(n * part, part), part)
            left = jnp.concatenate(
                [
                    held[pl.ds(first, 2), h, p].reshape(both, chunk)
                    for h in range(nm)
                    for p in range(pairs)
                ],
                axis=1,
            )
            product = jnp.dot(left, out_weight_ref[:, cols], preferred_element_type=jnp.float32)
            result = residual[pl.ds(first, 2), :, cols] + product.reshape(2, patches, part)
            outgoing[pl.ds(first, 2), :, cols] = result.astype(outgoing.dtype)
            smoothed_ref[:, cols] += jnp.sum(result, axis=0) * (1.0 / nd)

    gather.wait_slot(gather.sibling)
    steps = len(gather.order)
    project(gather.chip)
    give(gather.sibling).start()
    incoming[me] = outgoing[me]

    def finish_chip(step):
        gather.arrive_sibling(step)
        chip = gather.order[step]
        project(chip)
        for core in range(2):
            give(chip * 2 + core).start()

    if gather.relay:
        gather.arrive(0)
        gather.arrive(1)
        finish_chip(0)
        finish_chip(1)
        gather.arrive(2)
        finish_chip(2)
    else:
        for step in range(steps):
            gather.arrive(step)
        for step in range(steps):
            finish_chip(step)
    gather.finish()

    features_ref[:, pl.ds(pl.multiple_of(me * width, HEAD_DIM), width)] = incoming[me]
    for step in range(1, nd):
        source = lax.rem(me + step, nd)
        give(source).wait_send()
        remote(
            outgoing.at[source], incoming.at[source], f_send.at[source], f_recv.at[source],
            "dp", source,
        ).wait_recv()
        features_ref[:, pl.ds(pl.multiple_of(source * width, HEAD_DIM), width)] = incoming[source]


VMEM = pl.BlockSpec(memory_space=pltpu.VMEM)
DMA = pltpu.SemaphoreType.DMA


def on_device(
    clean_image, noise_draw, embed_weight, position_table, norm_gain, qkv_weight,
    query_gain, key_gain, out_weight,
):
    nd, nm = lax.axis_size("dp"), lax.axis_size("mp")
    patches, features = position_table.shape
    pixels, width = embed_weight.shape
    group = qkv_weight.shape[2]
    heads = group // HEAD_DIM
    chunk = HEAD_DIM * (2 if heads % 2 == 0 else 1)
    pairs = group // chunk
    rows, rows_full = round_up(pixels, 16), round_up(pixels, 128)
    me = lax.axis_index("dp")

    own_columns = lax.dynamic_slice_in_dim(out_weight, me * width, width, axis=1)
    out_columns = lax.all_gather(own_columns, "mp", axis=0, tiled=True)
    noisy = (
        clean_image[0].astype(jnp.float32) + 0.5 * noise_draw[0, 0].astype(jnp.float32)
    ).astype(jnp.bfloat16)
    noisy = jnp.pad(noisy.T, ((0, 0), (0, rows_full - pixels)))
    embed_padded = jnp.pad(embed_weight, ((0, rows - pixels), (0, 0)))
    noisy_copies = lax.all_gather(noisy[None], "dp", axis=0, tiled=True)

    bf16, f32 = jnp.bfloat16, jnp.float32
    total = nm * patches
    head_out = pl.pallas_call(
        functools.partial(heads_kernel, nd, nm),
        out_shape=jax.ShapeDtypeStruct((nm, pairs, patches, chunk), bf16),
        in_specs=[VMEM] * 4 + [pl.BlockSpec(memory_space=pl.ANY)] + [VMEM] * 2,
        out_specs=VMEM,
        scratch_shapes=[
            pltpu.VMEM((nm, patches, rows_full), bf16),
            pltpu.VMEM((nd, rows_full, width), bf16),
            pltpu.VMEM((nd, total, width), f32),
            pltpu.VMEM((nd, total, width), bf16),
            pltpu.VMEM((3, features, chunk), bf16),
            pltpu.VMEM((3, total, chunk), f32),
            pltpu.VMEM((pairs, nm, patches, chunk), bf16),
            pltpu.VMEM((nm, pairs, patches, chunk), bf16),
            DMA((nm,)), DMA((nm,)),
            DMA((sends(nd),)), DMA((nd,)), DMA((2,)),
            DMA((pairs, nm)), DMA((pairs, nm)),
            DMA((3,)),
        ],
        compiler_params=pltpu.CompilerParams(
            collective_id=0, has_side_effects=True, vmem_limit_bytes=60 * 1024 * 1024
        ),
        cost_estimate=pl.CostEstimate(
            flops=2 * total * features * 4 * group, bytes_accessed=qkv_weight.size * 2,
            transcendentals=0,
        ),
        name="embed_and_heads",
    )(
        noisy,
        embed_padded,
        position_table,
        norm_gain.reshape(nd, 1, width),
        jnp.transpose(qkv_weight, (1, 0, 2)),
        query_gain.reshape(1, HEAD_DIM),
        key_gain.reshape(1, HEAD_DIM),
    )

    own_position = lax.dynamic_slice_in_dim(position_table, me * width, width, axis=1)
    embed_full = jnp.pad(embed_weight, ((0, rows_full - pixels), (0, 0)))
    features_out, smoothed = pl.pallas_call(
        functools.partial(output_kernel, nd),
        out_shape=(
            jax.ShapeDtypeStruct((patches, features), bf16),
            jax.ShapeDtypeStruct((patches, width), f32),
        ),
        in_specs=[VMEM] * 5,
        out_specs=(VMEM, VMEM),
        scratch_shapes=[
            pltpu.VMEM((nd, nm, pairs, patches, chunk), bf16),
            pltpu.VMEM((nd, patches, width), f32),
            pltpu.VMEM((nd, patches, width), bf16),
            pltpu.VMEM((nd, patches, width), bf16),
            DMA((sends(nd),)), DMA((nd,)), DMA((2,)),
            DMA((nd,)), DMA((nd,)),
        ],
        compiler_params=pltpu.CompilerParams(
            collective_id=1, has_side_effects=True, vmem_limit_bytes=48 * 1024 * 1024
        ),
        cost_estimate=pl.CostEstimate(
            flops=2 * nd * patches * nm * group * width, bytes_accessed=2 * nm * group * width,
            transcendentals=0,
        ),
        name="project_and_share",
    )(head_out, noisy_copies, embed_full, own_position, out_columns)
    return features_out[:, None, None, :], smoothed[:, None, :]


def solution(mesh):
    placed = (
        P("mp", None, None),
        P("mp", "dp", None, None),
        P(None, "dp"),
        P(),
        P(),
        P(None, None, "mp"),
        P(),
        P(),
        P("mp", None),
    )
    return jax.shard_map(
        on_device,
        mesh=mesh,
        in_specs=placed,
        out_specs=(P(None, "dp", "mp", None), P(None, "mp", "dp")),
        check_vma=False,
    )
```

```python
import functools

import jax
import jax.numpy as jnp
from jax import lax
from jax.experimental import pallas as pl
from jax.experimental.pallas import tpu as pltpu
from jax.sharding import PartitionSpec as P

HEAD_DIM = 128
MESH = pl.DeviceIdType.MESH
EPSILON = 1e-06


def round_up(value, step):
    return (value + step - 1) // step * step


def remote(src, dst, send_sem, recv_sem, axis, target):
    return pltpu.make_async_remote_copy(
        src_ref=src,
        dst_ref=dst,
        send_sem=send_sem,
        recv_sem=recv_sem,
        device_id={axis: target},
        device_id_type=MESH,
    )


def greet(sizes):
    barrier = pltpu.get_barrier_semaphore()
    total = 0
    for axis, size in sizes:
        me = lax.axis_index(axis)
        for step in range(1, size):
            pl.semaphore_signal(
                barrier,
                inc=1,
                device_id={axis: lax.rem(me + step, size)},
                device_id_type=MESH,
            )
        total += size - 1
    pl.semaphore_wait(barrier, total)


class Gather:
    def __init__(self, size, own, slot, halves, send_sem, recv_sem, half_sem):
        self.size = size
        self.me = lax.axis_index("dp")
        self.core = lax.rem(self.me, 2)
        self.chip = self.me // 2
        self.chips = size // 2
        self.own, self.slot, self.halves = own, slot, halves
        self.send_sem, self.recv_sem, self.half_sem = send_sem, recv_sem, half_sem
        self.sent = []
        self.relay = self.chips == 4
        self.sibling = self.chip * 2 + 1 - self.core
        if self.relay:
            x = self.chip + 1 - 2 * lax.rem(self.chip, 2)
            y = lax.rem(self.chip + 2, 4)
            d = lax.rem(x + 2, 4)
            self.order = [x, y, d]
        else:
            self.order = [lax.rem(self.chip + j, self.chips) for j in range(1, self.chips)]

    def push(self, src, dst, recv, target):
        copy = remote(src, dst, self.send_sem.at[len(self.sent)], recv, "dp", target)
        copy.start()
        self.sent.append(copy)

    def start(self):
        me = self.me
        for chip in self.order[: 2 if self.relay else None]:
            self.push(self.own, self.slot(me), self.recv_sem.at[me], chip * 2 + self.core)
        self.push(self.own, self.slot(me), self.recv_sem.at[me], self.sibling)

    def wait_slot(self, source):
        there = self.slot(source)
        remote(there, there, self.send_sem.at[0], self.recv_sem.at[source], "dp", self.sibling).wait_recv()

    def to_sibling(self, source):
        there = self.slot(source)
        self.push(there, there, self.recv_sem.at[source], self.sibling)

    def arrive(self, step):
        source = self.order[step] * 2 + self.core
        if self.relay and step == 2:
            for half in range(2):
                part = self.halves(source, half)
                remote(part, part, self.send_sem.at[0], self.half_sem.at[half], "dp", self.sibling).wait_recv()
        else:
            self.wait_slot(source)
            if self.relay:
                part = self.halves(source, step)
                other = self.order[1 - step] * 2 + self.core
                self.push(part, part, self.half_sem.at[step], other)
        self.to_sibling(source)
        return source

    def arrive_sibling(self, step):
        source = self.order[step] * 2 + 1 - self.core
        self.wait_slot(source)
        return source

    def finish(self):
        for copy in self.sent:
            copy.wait_send()


def sends(size):
    chips = size // 2
    return (chips - 1) + 1 + (chips - 1) + 2


class Line:
    def __init__(self, size, own, slot, send_sem, recv_sem):
        self.size = size
        self.here = lax.axis_index("mp")
        self.own, self.slot = own, slot
        self.send_sem, self.recv_sem = send_sem, recv_sem

    def ways(self, hop):
        for side, step in enumerate((1, -1)):
            source = self.here - step * hop
            target = self.here + step
            held = (source >= 0) & (source < self.size)
            yield side, source, target, held, held & (target >= 0) & (target < self.size)

    def copy(self, hop, side, source, target):
        src = self.own if hop == 0 else self.slot(source)
        return remote(
            src, self.slot(source), self.send_sem.at[hop, side], self.recv_sem.at[source], "mp", target
        )

    def hop(self, hop):
        for side, source, target, held, onward in self.ways(hop):
            if hop > 0:
                @pl.when(held)
                def _():
                    self.copy(hop, side, source, target).wait_recv()

            if hop < self.size - 1:
                @pl.when(onward)
                def _():
                    self.copy(hop, side, source, target).start()

    def finish(self):
        for hop in range(self.size - 1):
            for side, source, target, _, onward in self.ways(hop):
                @pl.when(onward)
                def _():
                    self.copy(hop, side, source, target).wait_send()


def heads_kernel(
    nd, nm, clean_ref, noise_ref, embed_ref, position_ref, gain_ref, qgain_ref, kgain_ref,
    qkv_ref, out_weight_ref, held_ref, columns_ref, copies_ref,
    raised, pixels, blocks, embedded, means, squares, normed, weights, projected, outgoing,
    z_send, z_recv, w_send, w_recv, w_half, h_send, h_recv, g_send, g_recv, g_half,
    o_send, o_recv, c_send, c_recv, load_sem, own_sem,
):
    me = lax.axis_index("dp")
    here = lax.axis_index("mp")
    patches = position_ref.shape[0]
    width = embed_ref.shape[1]
    rows, rows_full = embed_ref.shape[0], blocks.shape[1]
    count = clean_ref.shape[0]
    total = nm * patches
    features = nd * width
    pairs, chunk = outgoing.shape[0], outgoing.shape[3]
    heads = chunk // HEAD_DIM

    def load(kind, pair):
        return pltpu.make_async_copy(
            qkv_ref.at[kind, :, pl.ds(pair * chunk, chunk)], weights.at[kind], load_sem.at[kind]
        )

    for kind in range(3):
        load(kind, 0).start()
    own_columns = out_weight_ref.at[:, pl.ds(pl.multiple_of(me * width, HEAD_DIM), width)]
    keep = [pltpu.make_async_copy(own_columns, columns_ref.at[here], own_sem.at[0])]
    keep[0].start()
    raised[...] = jnp.zeros_like(raised)
    raised[:count, :] = clean_ref[...].astype(jnp.float32) + 0.5 * noise_ref[...].astype(jnp.float32)
    pixels[here] = raised[...].T.astype(pixels.dtype)
    if rows_full > rows:
        blocks[:, rows:, :] = jnp.zeros((nd, rows_full - rows, width), blocks.dtype)
    greet((("dp", nd), ("mp", nm)))

    def pixel_copy(step):
        target = lax.rem(here + step, nm)
        return remote(
            pixels.at[here], pixels.at[here], z_send.at[step - 1], z_recv.at[here], "mp", target
        )

    for step in range(1, nm):
        pixel_copy(step).start()
    gather = Gather(
        nd,
        embed_ref,
        lambda s: blocks.at[s, pl.ds(0, rows)],
        lambda s, half: blocks.at[s, pl.ds(0, rows), pl.ds(half * (width // 2), width // 2)],
        w_send, w_recv, w_half,
    )
    gather.start()
    line = Line(nm, own_columns, lambda s: columns_ref.at[s], o_send, o_recv)
    line.hop(0)
    blocks[me, :rows, :] = embed_ref[...]
    for step in range(1, nm):
        source = lax.rem(here + step, nm)
        remote(
            pixels.at[here], pixels.at[source], z_send.at[0], z_recv.at[source], "mp", source
        ).wait_recv()

    part = 256 if width % 256 == 0 else 128
    band = 64

    done = []

    def embed(source):
        before = len(done)
        done.append(source)

        @pl.loop(0, width // part)
        def _(n):
            cols = pl.ds(pl.multiple_of(n * part, part), part)
            product = jnp.dot(
                pixels[...].reshape(total, rows_full),
                blocks[source, :, cols],
                preferred_element_type=jnp.float32,
            )
            place = position_ref[:, pl.ds(pl.multiple_of(source * width + n * part, part), part)]
            product = product.reshape(nm, patches, part) + place.astype(jnp.float32)[None]
            embedded[source, :, cols] = product.reshape(total, part)

        @pl.loop(0, total // band)
        def _(r):
            at = pl.ds(pl.multiple_of(r * band, band), band)
            values = embedded[source, at, :]
            mean = jnp.mean(values, axis=-1, keepdims=True)
            centred = values - mean
            square = jnp.sum(centred * centred, axis=-1, keepdims=True)
            if before == 0:
                means[at, :] = mean
                squares[at, :] = square
            else:
                apart = mean - means[at, :]
                means[at, :] += apart * (1.0 / (before + 1))
                squares[at, :] += square + apart * apart * (width * before / (before + 1))

    embed(me)
    steps = len(gather.order)
    gather.wait_slot(gather.sibling)
    embed(gather.sibling)
    if gather.relay:
        near = [gather.arrive(0), gather.arrive(1)]
        for source in near:
            embed(source)
        for step in range(2):
            embed(gather.arrive_sibling(step))
        far = gather.arrive(2)
        line.hop(1)
        embed(far)
        embed(gather.arrive_sibling(2))
    else:
        for step in range(steps):
            embed(gather.arrive(step))
        if nm > 1:
            line.hop(1)
        for step in range(steps):
            embed(gather.arrive_sibling(step))

    def copy_pixels(step):
        return remote(
            pixels.at[here], copies_ref.at[me], c_send.at[step - 1], c_recv.at[me], "dp",
            lax.rem(me + step, nd),
        )

    for step in range(1, nd):
        copy_pixels(step).start()
    keep.append(pltpu.make_async_copy(pixels.at[here], copies_ref.at[me], own_sem.at[1]))
    keep[1].start()

    @pl.loop(0, total // band)
    def _(r):
        at = pl.ds(pl.multiple_of(r * band, band), band)
        mean = means[at, :]
        scale = lax.rsqrt(squares[at, :] * (1.0 / features) + EPSILON)
        for s in range(nd):
            normed[at, s * width : (s + 1) * width] = (
                (embedded[s, at, :] - mean) * scale * gain_ref[s]
            ).astype(normed.dtype)

    def head_norm(values, gain):
        mean = jnp.mean(values, axis=-1, keepdims=True)
        centred = values - mean
        variance = jnp.mean(centred * centred, axis=-1, keepdims=True)
        return (centred * lax.rsqrt(variance + EPSILON) * gain[...]).astype(jnp.bfloat16)

    def exchange(pair, step):
        target = lax.rem(here + step, nm)
        return remote(
            outgoing.at[pair, target], held_ref.at[me, pair, here],
            h_send.at[pair, step - 1], h_recv.at[pair, here], "mp", target,
        )

    def keep_heads(pair):
        return pltpu.make_async_copy(
            outgoing.at[pair, here], held_ref.at[me, pair, here], own_sem.at[2 + pair]
        )

    shares = []

    def share(pair):
        keep_heads(pair).wait()
        for step in range(1, nm):
            source = lax.rem(here + step, nm)
            remote(
                outgoing.at[pair, source], held_ref.at[me, pair, source],
                h_send.at[pair, step - 1], h_recv.at[pair, source], "mp", source,
            ).wait_recv()
        shares.append(
            Gather(
                nd,
                held_ref.at[me, pair],
                lambda s: held_ref.at[s, pair],
                lambda s, half: held_ref.at[s, pair, pl.ds(half * (nm // 2), nm // 2)],
                g_send.at[pair], g_recv.at[pair], g_half.at[pair],
            )
        )
        shares[pair].start()

    def pass_near(pair):
        for step in range(min(2, steps)):
            shares[pair].arrive(step)

    def pass_far(pair):
        for step in range(2, steps):
            shares[pair].arrive(step)

    for pair in range(pairs):
        for kind in range(3):
            load(kind, pair).wait()
            projected[kind] = jnp.dot(
                normed[...], weights[kind], preferred_element_type=jnp.float32
            )
            if pair + 1 < pairs:
                load(kind, pair + 1).start()
            if kind == 1:
                if pair >= 2:
                    pass_far(pair - 2)
                if pair >= 1:
                    share(pair - 1)

        for image in range(nm):
            at = slice(image * patches, (image + 1) * patches)
            for head in range(heads):
                cols = slice(head * HEAD_DIM, (head + 1) * HEAD_DIM)
                query = head_norm(projected[0, at, cols], qgain_ref)
                key = head_norm(projected[1, at, cols], kgain_ref)
                value = projected[2, at, cols].astype(jnp.bfloat16)
                scores = lax.dot_general(
                    query, key, (((1,), (1,)), ((), ())), preferred_element_type=jnp.float32
                ) * HEAD_DIM ** (-0.5)
                powers = jnp.exp(scores)
                probs = (powers / jnp.sum(powers, axis=-1, keepdims=True)).astype(jnp.bfloat16)
                result = jnp.dot(probs, value, preferred_element_type=jnp.float32)
                outgoing[pair, image, :, cols] = result.astype(jnp.bfloat16)

        for step in range(1, nm):
            exchange(pair, step).start()
        keep_heads(pair).start()
        if pair == 0 and nm > 2:
            line.hop(2)
        if pair >= 1:
            pass_near(pair - 1)

    last = pairs - 1
    share(last)
    if last >= 1:
        pass_far(last - 1)
    pass_near(last)
    pass_far(last)

    for copy in keep:
        copy.wait()
    for hop in range(3, nm + 1):
        line.hop(hop)
    line.finish()
    for step in range(1, nm):
        pixel_copy(step).wait_send()
    for step in range(1, nd):
        copy_pixels(step).wait_send()
        source = lax.rem(me + step, nd)
        remote(
            pixels.at[here], copies_ref.at[source], c_send.at[0], c_recv.at[source], "dp", source
        ).wait_recv()
    gather.finish()
    for pair in range(pairs):
        for step in range(1, nm):
            exchange(pair, step).wait_send()
        for step in range(steps):
            shares[pair].arrive_sibling(step)
        shares[pair].wait_slot(shares[pair].sibling)
        shares[pair].finish()


def output_kernel(
    nd, heads_ref, noisy_ref, embed_ref, position_ref, out_weight_ref, features_ref, smoothed_ref,
    outgoing, incoming, f_send, f_recv,
):
    me = lax.axis_index("dp")
    _, pairs, nm, patches, chunk = heads_ref.shape
    width = embed_ref.shape[1]
    rows, rows_full = embed_ref.shape[0], noisy_ref.shape[2]
    greet((("dp", nd),))
    start = pl.ds(pl.multiple_of(me * width, HEAD_DIM), width)
    smoothed_ref[...] = jnp.zeros_like(smoothed_ref)
    part = 256 if width % 256 == 0 else 128
    both = 2 * patches

    def give(copy):
        return remote(
            outgoing.at[copy], incoming.at[me], f_send.at[copy], f_recv.at[me], "dp", copy
        )

    def project(chip):
        first = chip * 2

        @pl.loop(0, width // part)
        def _(n):
            cols = pl.ds(pl.multiple_of(n * part, part), part)
            left = jnp.concatenate(
                [
                    heads_ref[pl.ds(first, 2), p, h].reshape(both, chunk)
                    for h in range(nm)
                    for p in range(pairs)
                ],
                axis=1,
            )
            product = jnp.dot(
                left, out_weight_ref[:, cols], preferred_element_type=jnp.float32
            )
            noisy = noisy_ref[pl.ds(first, 2)].reshape(both, rows_full)[:, :rows]
            base = jnp.dot(noisy, embed_ref[:, cols], preferred_element_type=jnp.float32)
            place = position_ref[:, pl.ds(pl.multiple_of(me * width + n * part, part), part)]
            result = (product + base).reshape(2, patches, part) + place.astype(jnp.float32)[None]
            outgoing[pl.ds(first, 2), :, cols] = result.astype(outgoing.dtype)
            smoothed_ref[:, cols] += jnp.sum(result, axis=0) * (1.0 / nd)

    here = me // 2
    chips = nd // 2
    for step in range(1, chips):
        chip = lax.rem(here + step, chips)
        project(chip)
        for core in range(2):
            give(chip * 2 + core).start()
    project(here)
    sibling = here * 2 + 1 - lax.rem(me, 2)
    give(sibling).start()
    features_ref[:, start] = outgoing[me]
    for step in range(1, nd):
        source = lax.rem(me + step, nd)
        give(source).wait_send()
        remote(
            outgoing.at[source], incoming.at[source], f_send.at[source], f_recv.at[source],
            "dp", source,
        ).wait_recv()
        features_ref[:, pl.ds(pl.multiple_of(source * width, HEAD_DIM), width)] = incoming[source]


VMEM = pl.BlockSpec(memory_space=pltpu.VMEM)
DMA = pltpu.SemaphoreType.DMA


def on_device(
    clean_image, noise_draw, embed_weight, position_table, norm_gain, qkv_weight,
    query_gain, key_gain, out_weight,
):
    nd, nm = lax.axis_size("dp"), lax.axis_size("mp")
    patches, features = position_table.shape
    pixels, width = embed_weight.shape
    group = qkv_weight.shape[2]
    heads = group // HEAD_DIM
    chunk = HEAD_DIM * (2 if heads % 2 == 0 else 1)
    pairs = group // chunk
    rows, rows_full = round_up(pixels, 16), round_up(pixels, 128)

    embed_padded = jnp.pad(embed_weight, ((0, rows - pixels), (0, 0)))

    bf16, f32 = jnp.bfloat16, jnp.float32
    total = nm * patches
    anywhere = pl.BlockSpec(memory_space=pl.ANY)
    held, columns, copies = pl.pallas_call(
        functools.partial(heads_kernel, nd, nm),
        out_shape=(
            jax.ShapeDtypeStruct((nd, pairs, nm, patches, chunk), bf16),
            jax.ShapeDtypeStruct((nm, group, width), bf16),
            jax.ShapeDtypeStruct((nd, patches, rows_full), bf16),
        ),
        in_specs=[VMEM] * 7 + [anywhere] * 2,
        out_specs=(anywhere,) * 3,
        scratch_shapes=[
            pltpu.VMEM((rows_full, patches), f32),
            pltpu.VMEM((nm, patches, rows_full), bf16),
            pltpu.VMEM((nd, rows_full, width), bf16),
            pltpu.VMEM((nd, total, width), f32),
            pltpu.VMEM((total, 1), f32),
            pltpu.VMEM((total, 1), f32),
            pltpu.VMEM((total, features), bf16),
            pltpu.VMEM((3, features, chunk), bf16),
            pltpu.VMEM((3, total, chunk), f32),
            pltpu.VMEM((pairs, nm, patches, chunk), bf16),
            DMA((nm,)), DMA((nm,)),
            DMA((sends(nd),)), DMA((nd,)), DMA((2,)),
            DMA((pairs, nm)), DMA((pairs, nm)),
            DMA((pairs, sends(nd))), DMA((pairs, nd)), DMA((pairs, 2)),
            DMA((nm, 2)), DMA((nm,)),
            DMA((nd,)), DMA((nd,)),
            DMA((3,)), DMA((2 + pairs,)),
        ],
        compiler_params=pltpu.CompilerParams(
            collective_id=0, has_side_effects=True, vmem_limit_bytes=62 * 1024 * 1024
        ),
        cost_estimate=pl.CostEstimate(
            flops=2 * total * features * 4 * group, bytes_accessed=qkv_weight.size * 2,
            transcendentals=0,
        ),
        name="embed_and_heads",
    )(
        clean_image[0],
        noise_draw[0, 0],
        embed_padded,
        position_table,
        norm_gain.reshape(nd, 1, width),
        query_gain.reshape(1, HEAD_DIM),
        key_gain.reshape(1, HEAD_DIM),
        jnp.transpose(qkv_weight, (1, 0, 2)),
        out_weight,
    )

    features_out, smoothed = pl.pallas_call(
        functools.partial(output_kernel, nd),
        out_shape=(
            jax.ShapeDtypeStruct((patches, features), bf16),
            jax.ShapeDtypeStruct((patches, width), f32),
        ),
        in_specs=[VMEM] * 5,
        out_specs=(VMEM, VMEM),
        scratch_shapes=[
            pltpu.VMEM((nd, patches, width), bf16),
            pltpu.VMEM((nd, patches, width), bf16),
            DMA((nd,)), DMA((nd,)),
        ],
        compiler_params=pltpu.CompilerParams(
            collective_id=1, has_side_effects=True, vmem_limit_bytes=48 * 1024 * 1024
        ),
        cost_estimate=pl.CostEstimate(
            flops=2 * nd * patches * nm * group * width, bytes_accessed=2 * nm * group * width,
            transcendentals=0,
        ),
        name="project_and_share",
    )(held, copies, embed_padded, position_table, columns.reshape(nm * group, width))
    return features_out[:, None, None, :], smoothed[:, None, :]


def solution(mesh):
    placed = (
        P("mp", None, None),
        P("mp", "dp", None, None),
        P(None, "dp"),
        P(),
        P(),
        P(None, None, "mp"),
        P(),
        P(),
        P("mp", None),
    )
    return jax.shard_map(
        on_device,
        mesh=mesh,
        in_specs=placed,
        out_specs=(P(None, "dp", "mp", None), P(None, "mp", "dp")),
        check_vma=False,
    )
```

```python
import functools

import jax
import jax.numpy as jnp
from jax import lax
from jax.experimental import pallas as pl
from jax.experimental.pallas import tpu as pltpu
from jax.sharding import PartitionSpec as P

HEAD_DIM = 128
MESH = pl.DeviceIdType.MESH
EPSILON = 1e-06


def round_up(value, step):
    return (value + step - 1) // step * step


def remote(src, dst, send_sem, recv_sem, axis, target):
    return pltpu.make_async_remote_copy(
        src_ref=src,
        dst_ref=dst,
        send_sem=send_sem,
        recv_sem=recv_sem,
        device_id={axis: target},
        device_id_type=MESH,
    )


def greet(sizes):
    barrier = pltpu.get_barrier_semaphore()
    total = 0
    for axis, size in sizes:
        me = lax.axis_index(axis)
        for step in range(1, size):
            pl.semaphore_signal(
                barrier,
                inc=1,
                device_id={axis: lax.rem(me + step, size)},
                device_id_type=MESH,
            )
        total += size - 1
    pl.semaphore_wait(barrier, total)


class Gather:
    def __init__(self, size, own, slot, halves, send_sem, recv_sem, half_sem):
        self.size = size
        self.me = lax.axis_index("dp")
        self.core = lax.rem(self.me, 2)
        self.chip = self.me // 2
        self.chips = size // 2
        self.own, self.slot, self.halves = own, slot, halves
        self.send_sem, self.recv_sem, self.half_sem = send_sem, recv_sem, half_sem
        self.sent = []
        self.relay = self.chips == 4
        self.sibling = self.chip * 2 + 1 - self.core
        if self.relay:
            x = self.chip + 1 - 2 * lax.rem(self.chip, 2)
            y = lax.rem(self.chip + 2, 4)
            d = lax.rem(x + 2, 4)
            self.order = [x, y, d]
        else:
            self.order = [lax.rem(self.chip + j, self.chips) for j in range(1, self.chips)]

    def push(self, src, dst, recv, target):
        copy = remote(src, dst, self.send_sem.at[len(self.sent)], recv, "dp", target)
        copy.start()
        self.sent.append(copy)

    def start(self):
        me = self.me
        for chip in self.order[: 2 if self.relay else None]:
            self.push(self.own, self.slot(me), self.recv_sem.at[me], chip * 2 + self.core)
        self.push(self.own, self.slot(me), self.recv_sem.at[me], self.sibling)

    def wait_slot(self, source):
        there = self.slot(source)
        remote(there, there, self.send_sem.at[0], self.recv_sem.at[source], "dp", self.sibling).wait_recv()

    def to_sibling(self, source):
        there = self.slot(source)
        self.push(there, there, self.recv_sem.at[source], self.sibling)

    def arrive(self, step):
        source = self.order[step] * 2 + self.core
        if self.relay and step == 2:
            for half in range(2):
                part = self.halves(source, half)
                remote(part, part, self.send_sem.at[0], self.half_sem.at[half], "dp", self.sibling).wait_recv()
        else:
            self.wait_slot(source)
            if self.relay:
                part = self.halves(source, step)
                other = self.order[1 - step] * 2 + self.core
                self.push(part, part, self.half_sem.at[step], other)
        self.to_sibling(source)
        return source

    def arrive_sibling(self, step):
        source = self.order[step] * 2 + 1 - self.core
        self.wait_slot(source)
        return source

    def finish(self):
        for copy in self.sent:
            copy.wait_send()


def sends(size):
    chips = size // 2
    return (chips - 1) + 1 + (chips - 1) + 2


def late_panel(size):
    return size > 2


def panel_width(width):
    return 256 if width % 256 == 0 else 128


class Line:
    def __init__(self, size, own, slot, early, send_sem, recv_sem):
        self.size = size
        self.here = lax.axis_index("mp")
        self.early = early
        self.own, self.slot = own, slot
        self.send_sem, self.recv_sem = send_sem, recv_sem

    def ways(self, hop):
        for side, step in enumerate((1, -1)):
            source = self.here - step * hop
            target = self.here + step
            held = (source >= 0) & (source < self.size)
            yield side, source, target, held, held & (target >= 0) & (target < self.size)

    def copy(self, hop, side, source, target):
        src, dst = self.own if hop == 0 else self.slot(source), self.slot(source)
        if late_panel(self.size) and hop == self.size - 2:
            src, dst = src.at[:, self.early], dst.at[:, self.early]
        return remote(
            src, dst, self.send_sem.at[hop, side], self.recv_sem.at[source], "mp", target
        )

    def hop(self, hop):
        for side, source, target, held, onward in self.ways(hop):
            if hop > 0:
                @pl.when(held)
                def _():
                    self.copy(hop - 1, side, source, target).wait_recv()

            if hop < self.size - 1:
                @pl.when(onward)
                def _():
                    self.copy(hop, side, source, target).start()

    def finish(self):
        for hop in range(self.size - 1):
            for side, source, target, _, onward in self.ways(hop):
                @pl.when(onward)
                def _():
                    self.copy(hop, side, source, target).wait_send()


def heads_kernel(
    nd, nm, clean_ref, noise_ref, embed_ref, position_ref, gain_ref, qgain_ref, kgain_ref,
    qkv_ref, out_weight_ref, held_ref, columns_ref, copies_ref,
    raised, pixels, blocks, embedded, means, squares, normed, weights, projected, outgoing,
    z_send, z_recv, w_send, w_recv, w_half, h_send, h_recv, g_send, g_recv, g_half,
    o_send, o_recv, c_send, c_recv, load_sem, own_sem,
):
    me = lax.axis_index("dp")
    here = lax.axis_index("mp")
    patches = position_ref.shape[0]
    width = embed_ref.shape[1]
    count, rows_full = clean_ref.shape[0], blocks.shape[1]
    rows = round_up(count, 16)
    tail = count // 16 * 16
    total = nm * patches
    features = nd * width
    pairs, chunk = outgoing.shape[0], outgoing.shape[3]
    heads = chunk // HEAD_DIM

    def load(kind, pair):
        return pltpu.make_async_copy(
            qkv_ref.at[kind, :, pl.ds(pair * chunk, chunk)], weights.at[kind], load_sem.at[kind]
        )

    for kind in range(3):
        load(kind, 0).start()
    own_columns = out_weight_ref.at[:, pl.ds(pl.multiple_of(me * width, HEAD_DIM), width)]
    keep = [pltpu.make_async_copy(own_columns, columns_ref.at[here], own_sem.at[0])]
    keep[0].start()
    raised[...] = jnp.zeros_like(raised)
    raised[:count, :] = clean_ref[...].astype(jnp.float32) + 0.5 * noise_ref[...].astype(jnp.float32)
    pixels[here] = raised[...].T.astype(pixels.dtype)
    if rows_full > tail:
        blocks[:, tail:, :] = jnp.zeros((nd, rows_full - tail, width), blocks.dtype)
    blocks[me, :count, :] = embed_ref[...]
    greet((("dp", nd), ("mp", nm)))

    def pixel_copy(step):
        target = lax.rem(here + step, nm)
        return remote(
            pixels.at[here], pixels.at[here], z_send.at[step - 1], z_recv.at[here], "mp", target
        )

    for step in range(1, nm):
        pixel_copy(step).start()
    gather = Gather(
        nd,
        blocks.at[me, pl.ds(0, rows)],
        lambda s: blocks.at[s, pl.ds(0, rows)],
        lambda s, half: blocks.at[s, pl.ds(0, rows), pl.ds(half * (width // 2), width // 2)],
        w_send, w_recv, w_half,
    )
    gather.start()
    part = panel_width(width)
    early = pl.ds(0, width - part)
    line = Line(nm, own_columns, lambda s: columns_ref.at[s], early, o_send, o_recv)
    line.hop(0)
    for step in range(1, nm):
        source = lax.rem(here + step, nm)
        remote(
            pixels.at[here], pixels.at[source], z_send.at[0], z_recv.at[source], "mp", source
        ).wait_recv()

    band = 64

    done = []

    def embed(source):
        before = len(done)
        done.append(source)

        @pl.loop(0, width // part)
        def _(n):
            cols = pl.ds(pl.multiple_of(n * part, part), part)
            product = jnp.dot(
                pixels[...].reshape(total, rows_full),
                blocks[source, :, cols],
                preferred_element_type=jnp.float32,
            )
            place = position_ref[:, pl.ds(pl.multiple_of(source * width + n * part, part), part)]
            product = product.reshape(nm, patches, part) + place.astype(jnp.float32)[None]
            embedded[source, :, cols] = product.reshape(total, part)

        @pl.loop(0, total // band)
        def _(r):
            at = pl.ds(pl.multiple_of(r * band, band), band)
            values = embedded[source, at, :]
            mean = jnp.mean(values, axis=-1, keepdims=True)
            centred = values - mean
            square = jnp.sum(centred * centred, axis=-1, keepdims=True)
            if before == 0:
                means[at, :] = mean
                squares[at, :] = square
            else:
                apart = mean - means[at, :]
                means[at, :] += apart * (1.0 / (before + 1))
                squares[at, :] += square + apart * apart * (width * before / (before + 1))

    embed(me)
    steps = len(gather.order)
    gather.wait_slot(gather.sibling)
    embed(gather.sibling)
    if gather.relay:
        near = [gather.arrive(0), gather.arrive(1)]
        for source in near:
            embed(source)
        for step in range(2):
            embed(gather.arrive_sibling(step))
        far = gather.arrive(2)
        embed(far)
        line.hop(1)
        embed(gather.arrive_sibling(2))
    else:
        for step in range(steps):
            embed(gather.arrive(step))
        if nm > 1:
            line.hop(1)
        for step in range(steps):
            embed(gather.arrive_sibling(step))

    def copy_pixels(step):
        return remote(
            pixels.at[here], copies_ref.at[me], c_send.at[step - 1], c_recv.at[me], "dp",
            lax.rem(me + step, nd),
        )

    for step in range(1, nd):
        copy_pixels(step).start()
    keep.append(pltpu.make_async_copy(pixels.at[here], copies_ref.at[me], own_sem.at[1]))
    keep[1].start()

    @pl.loop(0, total // band)
    def _(r):
        at = pl.ds(pl.multiple_of(r * band, band), band)
        mean = means[at, :]
        scale = lax.rsqrt(squares[at, :] * (1.0 / features) + EPSILON)
        for s in range(nd):
            normed[at, s * width : (s + 1) * width] = (
                (embedded[s, at, :] - mean) * scale * gain_ref[s]
            ).astype(normed.dtype)

    def head_norm(values, gain):
        mean = jnp.mean(values, axis=-1, keepdims=True)
        centred = values - mean
        variance = jnp.mean(centred * centred, axis=-1, keepdims=True)
        return (centred * lax.rsqrt(variance + EPSILON) * gain[...]).astype(jnp.bfloat16)

    def exchange(pair, step):
        target = lax.rem(here + step, nm)
        return remote(
            outgoing.at[pair, target], held_ref.at[me, pair, here],
            h_send.at[pair, step - 1], h_recv.at[pair, here], "mp", target,
        )

    def keep_heads(pair):
        return pltpu.make_async_copy(
            outgoing.at[pair, here], held_ref.at[me, pair, here], own_sem.at[2 + pair]
        )

    shares = []

    def share(pair):
        keep_heads(pair).wait()
        for step in range(1, nm):
            source = lax.rem(here + step, nm)
            remote(
                outgoing.at[pair, source], held_ref.at[me, pair, source],
                h_send.at[pair, step - 1], h_recv.at[pair, source], "mp", source,
            ).wait_recv()
        shares.append(
            Gather(
                nd,
                held_ref.at[me, pair],
                lambda s: held_ref.at[s, pair],
                lambda s, half: held_ref.at[s, pair, pl.ds(half * (nm // 2), nm // 2)],
                g_send.at[pair], g_recv.at[pair], g_half.at[pair],
            )
        )
        shares[pair].start()

    def pass_near(pair):
        for step in range(min(2, steps)):
            shares[pair].arrive(step)

    def pass_far(pair):
        for step in range(2, steps):
            shares[pair].arrive(step)

    for pair in range(pairs):
        for kind in range(3):
            load(kind, pair).wait()
            projected[kind] = jnp.dot(
                normed[...], weights[kind], preferred_element_type=jnp.float32
            )
            if pair + 1 < pairs:
                load(kind, pair + 1).start()
            if kind == 1:
                if pair == min(1, pairs - 1):
                    for hop in range(2, min(3, nm)):
                        line.hop(hop)
                if pair >= 2:
                    pass_far(pair - 2)
                if pair >= 1:
                    share(pair - 1)

        for image in range(nm):
            at = slice(image * patches, (image + 1) * patches)
            for head in range(heads):
                cols = slice(head * HEAD_DIM, (head + 1) * HEAD_DIM)
                query = head_norm(projected[0, at, cols], qgain_ref)
                key = head_norm(projected[1, at, cols], kgain_ref)
                value = projected[2, at, cols].astype(jnp.bfloat16)
                scores = lax.dot_general(
                    query, key, (((1,), (1,)), ((), ())), preferred_element_type=jnp.float32
                ) * HEAD_DIM ** (-0.5)
                powers = jnp.exp(scores)
                probs = (powers / jnp.sum(powers, axis=-1, keepdims=True)).astype(jnp.bfloat16)
                result = jnp.dot(probs, value, preferred_element_type=jnp.float32)
                outgoing[pair, image, :, cols] = result.astype(jnp.bfloat16)

        for step in range(1, nm):
            exchange(pair, step).start()
        keep_heads(pair).start()
        if pair >= 1:
            pass_near(pair - 1)

    last = pairs - 1
    share(last)
    if last >= 1:
        pass_far(last - 1)
    pass_near(last)
    pass_far(last)

    for copy in keep:
        copy.wait()
    for hop in range(3, nm + 1):
        line.hop(hop)
    line.finish()
    for step in range(1, nm):
        pixel_copy(step).wait_send()
    for step in range(1, nd):
        copy_pixels(step).wait_send()
        source = lax.rem(me + step, nd)
        remote(
            pixels.at[here], copies_ref.at[source], c_send.at[0], c_recv.at[source], "dp", source
        ).wait_recv()
    gather.finish()
    for pair in range(pairs):
        for step in range(1, nm):
            exchange(pair, step).wait_send()
        for step in range(steps):
            shares[pair].arrive_sibling(step)
        shares[pair].wait_slot(shares[pair].sibling)
        shares[pair].finish()


def output_kernel(
    nd, nm, heads_ref, noisy_ref, embed_ref, position_ref, columns_ref, features_ref, smoothed_ref,
    weights, embed_full, outgoing, incoming, f_send, f_recv, late_send, late_recv, load_sem,
):
    me = lax.axis_index("dp")
    here = lax.axis_index("mp")
    _, pairs, _, patches, chunk = heads_ref.shape
    width = embed_ref.shape[1]
    count, rows_full = embed_ref.shape[0], noisy_ref.shape[2]
    group = columns_ref.shape[1]
    part = panel_width(width)
    panels = width // part
    early, late = pl.ds(0, width - part), pl.ds(width - part, part)
    both = 2 * patches

    first_load = pltpu.make_async_copy(
        columns_ref.at[:, :, early], weights.at[:, :, early], load_sem.at[nm]
    )
    first_load.start()

    def late_loads():
        for source in range(nm):
            near = (here - source < nm - 1) & (source - here < nm - 1)
            copy = pltpu.make_async_copy(
                columns_ref.at[source, :, late], weights.at[source, :, late], load_sem.at[source]
            )
            yield near if late_panel(nm) else here >= 0, copy

    for near, copy in late_loads():
        @pl.when(near)
        def _():
            copy.start()

    greet((("dp", nd), ("mp", nm)))

    def late_hop(side, step, source, target):
        return remote(
            columns_ref.at[source, :, late], weights.at[source, :, late],
            late_send.at[side], late_recv.at[side], "mp", target,
        )

    def late_sends():
        for side, step in enumerate((1, -1)):
            source, target = here - step * (nm - 2), here + step
            go = (source >= 0) & (source < nm) & (target >= 0) & (target < nm)
            yield go, late_hop(side, step, source, target)

    if late_panel(nm):
        for go, copy in late_sends():
            @pl.when(go)
            def _():
                copy.start()

    embed_full[count // 16 * 16 :, :] = jnp.zeros(
        (rows_full - count // 16 * 16, width), embed_full.dtype
    )
    embed_full[:count, :] = embed_ref[...]
    smoothed_ref[...] = jnp.zeros_like(smoothed_ref)

    def give(panel, copy):
        return remote(
            outgoing.at[panel, copy], incoming.at[panel, me],
            f_send.at[panel, copy], f_recv.at[panel, me], "dp", copy,
        )

    def project(panel, chip):
        pair = pl.ds(chip * 2, 2)
        cols = slice(panel * part, (panel + 1) * part)
        left = jnp.concatenate(
            [heads_ref[pair, p, h].reshape(both, chunk) for h in range(nm) for p in range(pairs)],
            axis=1,
        )
        product = jnp.dot(
            left, weights[:, :, cols].reshape(nm * group, part), preferred_element_type=jnp.float32
        )
        base = jnp.dot(
            noisy_ref[pair].reshape(both, rows_full), embed_full[:, cols],
            preferred_element_type=jnp.float32,
        )
        place = position_ref[:, pl.ds(pl.multiple_of(me * width + panel * part, part), part)]
        result = (product + base).reshape(2, patches, part) + place.astype(jnp.float32)[None]
        outgoing[panel, pair] = result.astype(outgoing.dtype)
        smoothed_ref[:, cols] += jnp.sum(result, axis=0) * (1.0 / nd)

    chip_here = me // 2
    chips = nd // 2
    sibling = chip_here * 2 + 1 - lax.rem(me, 2)
    first_load.wait()
    for panel in range(panels):
        if panel == panels - 1:
            for near, copy in late_loads():
                @pl.when(near)
                def _():
                    copy.wait()

            if late_panel(nm):
                for side, step in enumerate((1, -1)):
                    source = here - step * (nm - 1)

                    @pl.when((source >= 0) & (source < nm))
                    def _():
                        late_hop(side, step, source, here - step).wait_recv()

        for step in range(1, chips):
            chip = lax.rem(chip_here + step, chips)
            project(panel, chip)
            for core in range(2):
                give(panel, chip * 2 + core).start()
        project(panel, chip_here)
        give(panel, sibling).start()
        at = pl.ds(pl.multiple_of(me * width + panel * part, part), part)
        features_ref[:, at] = outgoing[panel, me]

    if late_panel(nm):
        for go, copy in late_sends():
            @pl.when(go)
            def _():
                copy.wait_send()

    for panel in range(panels):
        for step in range(1, nd):
            source = lax.rem(me + step, nd)
            give(panel, source).wait_send()
            remote(
                outgoing.at[panel, source], incoming.at[panel, source],
                f_send.at[panel, source], f_recv.at[panel, source], "dp", source,
            ).wait_recv()
            at = pl.ds(pl.multiple_of(source * width + panel * part, part), part)
            features_ref[:, at] = incoming[panel, source]


VMEM = pl.BlockSpec(memory_space=pltpu.VMEM)
DMA = pltpu.SemaphoreType.DMA


def on_device(
    clean_image, noise_draw, embed_weight, position_table, norm_gain, qkv_weight,
    query_gain, key_gain, out_weight,
):
    nd, nm = lax.axis_size("dp"), lax.axis_size("mp")
    patches, features = position_table.shape
    pixels, width = embed_weight.shape
    group = qkv_weight.shape[2]
    heads = group // HEAD_DIM
    chunk = HEAD_DIM * (2 if heads % 2 == 0 else 1)
    pairs = group // chunk
    rows_full = round_up(pixels, 128)

    part = panel_width(width)

    bf16, f32 = jnp.bfloat16, jnp.float32
    total = nm * patches
    anywhere = pl.BlockSpec(memory_space=pl.ANY)
    held, columns, copies = pl.pallas_call(
        functools.partial(heads_kernel, nd, nm),
        out_shape=(
            jax.ShapeDtypeStruct((nd, pairs, nm, patches, chunk), bf16),
            jax.ShapeDtypeStruct((nm, group, width), bf16),
            jax.ShapeDtypeStruct((nd, patches, rows_full), bf16),
        ),
        in_specs=[VMEM] * 7 + [anywhere] * 2,
        out_specs=(anywhere,) * 3,
        scratch_shapes=[
            pltpu.VMEM((rows_full, patches), f32),
            pltpu.VMEM((nm, patches, rows_full), bf16),
            pltpu.VMEM((nd, rows_full, width), bf16),
            pltpu.VMEM((nd, total, width), f32),
            pltpu.VMEM((total, 1), f32),
            pltpu.VMEM((total, 1), f32),
            pltpu.VMEM((total, features), bf16),
            pltpu.VMEM((3, features, chunk), bf16),
            pltpu.VMEM((3, total, chunk), f32),
            pltpu.VMEM((pairs, nm, patches, chunk), bf16),
            DMA((nm,)), DMA((nm,)),
            DMA((sends(nd),)), DMA((nd,)), DMA((2,)),
            DMA((pairs, nm)), DMA((pairs, nm)),
            DMA((pairs, sends(nd))), DMA((pairs, nd)), DMA((pairs, 2)),
            DMA((nm, 2)), DMA((nm,)),
            DMA((nd,)), DMA((nd,)),
            DMA((3,)), DMA((2 + pairs,)),
        ],
        compiler_params=pltpu.CompilerParams(
            collective_id=0, has_side_effects=True, vmem_limit_bytes=62 * 1024 * 1024
        ),
        cost_estimate=pl.CostEstimate(
            flops=2 * total * features * 4 * group, bytes_accessed=qkv_weight.size * 2,
            transcendentals=0,
        ),
        name="embed_and_heads",
    )(
        clean_image[0],
        noise_draw[0, 0],
        embed_weight,
        position_table,
        norm_gain.reshape(nd, 1, width),
        query_gain.reshape(1, HEAD_DIM),
        key_gain.reshape(1, HEAD_DIM),
        jnp.transpose(qkv_weight, (1, 0, 2)),
        out_weight,
    )

    features_out, smoothed = pl.pallas_call(
        functools.partial(output_kernel, nd, nm),
        out_shape=(
            jax.ShapeDtypeStruct((patches, features), bf16),
            jax.ShapeDtypeStruct((patches, width), f32),
        ),
        in_specs=[VMEM] * 4 + [anywhere],
        out_specs=(VMEM, VMEM),
        scratch_shapes=[
            pltpu.VMEM((nm, group, width), bf16),
            pltpu.VMEM((rows_full, width), bf16),
            pltpu.VMEM((width // part, nd, patches, part), bf16),
            pltpu.VMEM((width // part, nd, patches, part), bf16),
            DMA((width // part, nd)), DMA((width // part, nd)),
            DMA((2,)), DMA((2,)), DMA((nm + 1,)),
        ],
        compiler_params=pltpu.CompilerParams(
            collective_id=1, has_side_effects=True, vmem_limit_bytes=48 * 1024 * 1024
        ),
        cost_estimate=pl.CostEstimate(
            flops=2 * nd * patches * nm * group * width, bytes_accessed=2 * nm * group * width,
            transcendentals=0,
        ),
        name="project_and_share",
    )(held, copies, embed_weight, position_table, columns)
    return features_out[:, None, None, :], smoothed[:, None, :]


def solution(mesh):
    placed = (
        P("mp", None, None),
        P("mp", "dp", None, None),
        P(None, "dp"),
        P(),
        P(),
        P(None, None, "mp"),
        P(),
        P(),
        P("mp", None),
    )
    return jax.shard_map(
        on_device,
        mesh=mesh,
        in_specs=placed,
        out_specs=(P(None, "dp", "mp", None), P(None, "mp", "dp")),
        check_vma=False,
    )
```

```python
import functools

import jax
import jax.numpy as jnp
from jax import lax
from jax.experimental import pallas as pl
from jax.experimental.pallas import tpu as pltpu
from jax.sharding import PartitionSpec as P

HEAD_DIM = 128
MESH = pl.DeviceIdType.MESH
EPSILON = 1e-06


def round_up(value, step):
    return (value + step - 1) // step * step


def remote(src, dst, send_sem, recv_sem, axis, target):
    return pltpu.make_async_remote_copy(
        src_ref=src,
        dst_ref=dst,
        send_sem=send_sem,
        recv_sem=recv_sem,
        device_id={axis: target},
        device_id_type=MESH,
    )


def greet(sizes):
    barrier = pltpu.get_barrier_semaphore()
    total = 0
    for axis, size in sizes:
        me = lax.axis_index(axis)
        for step in range(1, size):
            pl.semaphore_signal(
                barrier,
                inc=1,
                device_id={axis: lax.rem(me + step, size)},
                device_id_type=MESH,
            )
        total += size - 1
    pl.semaphore_wait(barrier, total)


class Gather:
    def __init__(self, size, own, slot, halves, send_sem, recv_sem, half_sem):
        self.size = size
        self.me = lax.axis_index("dp")
        self.core = lax.rem(self.me, 2)
        self.chip = self.me // 2
        self.chips = size // 2
        self.own, self.slot, self.halves = own, slot, halves
        self.send_sem, self.recv_sem, self.half_sem = send_sem, recv_sem, half_sem
        self.sent = []
        self.relay = self.chips == 4
        self.sibling = self.chip * 2 + 1 - self.core
        if self.relay:
            x = self.chip + 1 - 2 * lax.rem(self.chip, 2)
            y = lax.rem(self.chip + 2, 4)
            d = lax.rem(x + 2, 4)
            self.order = [x, y, d]
        else:
            self.order = [lax.rem(self.chip + j, self.chips) for j in range(1, self.chips)]

    def push(self, src, dst, recv, target):
        copy = remote(src, dst, self.send_sem.at[len(self.sent)], recv, "dp", target)
        copy.start()
        self.sent.append(copy)

    def start(self):
        me = self.me
        for chip in self.order[: 2 if self.relay else None]:
            self.push(self.own, self.slot(me), self.recv_sem.at[me], chip * 2 + self.core)
        self.push(self.own, self.slot(me), self.recv_sem.at[me], self.sibling)

    def wait_slot(self, source):
        there = self.slot(source)
        remote(there, there, self.send_sem.at[0], self.recv_sem.at[source], "dp", self.sibling).wait_recv()

    def to_sibling(self, source):
        there = self.slot(source)
        self.push(there, there, self.recv_sem.at[source], self.sibling)

    def arrive(self, step):
        source = self.order[step] * 2 + self.core
        if self.relay and step == 2:
            for half in range(2):
                part = self.halves(source, half)
                remote(part, part, self.send_sem.at[0], self.half_sem.at[half], "dp", self.sibling).wait_recv()
        else:
            self.wait_slot(source)
            if self.relay:
                part = self.halves(source, step)
                other = self.order[1 - step] * 2 + self.core
                self.push(part, part, self.half_sem.at[step], other)
        self.to_sibling(source)
        return source

    def arrive_sibling(self, step):
        source = self.order[step] * 2 + 1 - self.core
        self.wait_slot(source)
        return source

    def finish(self):
        for copy in self.sent:
            copy.wait_send()


def sends(size):
    chips = size // 2
    return (chips - 1) + 1 + (chips - 1) + 2


def late_panel(size):
    return size > 2


def panel_width(width):
    return 256 if width % 256 == 0 else 128


class Line:
    def __init__(self, size, own, slot, early, send_sem, recv_sem):
        self.size = size
        self.here = lax.axis_index("mp")
        self.early = early
        self.own, self.slot = own, slot
        self.send_sem, self.recv_sem = send_sem, recv_sem

    def ways(self, hop):
        for side, step in enumerate((1, -1)):
            source = self.here - step * hop
            target = self.here + step
            held = (source >= 0) & (source < self.size)
            yield side, source, target, held, held & (target >= 0) & (target < self.size)

    def copy(self, hop, side, source, target):
        src, dst = self.own if hop == 0 else self.slot(source), self.slot(source)
        if late_panel(self.size) and hop == self.size - 2:
            src, dst = src.at[:, self.early], dst.at[:, self.early]
        return remote(
            src, dst, self.send_sem.at[hop, side], self.recv_sem.at[source], "mp", target
        )

    def hop(self, hop):
        for side, source, target, held, onward in self.ways(hop):
            if hop > 0:
                @pl.when(held)
                def _():
                    self.copy(hop - 1, side, source, target).wait_recv()

            if hop < self.size - 1:
                @pl.when(onward)
                def _():
                    self.copy(hop, side, source, target).start()

    def rest_copy(self, side, source, target):
        there = self.slot(source).at[:, self.second]
        return remote(
            there, there, self.rest_send.at[side], self.rest_recv.at[side], "mp", target
        )

    def rest(self):
        for side, source, target, _, onward in self.ways(self.size - 2):
            @pl.when(onward)
            def _():
                self.rest_copy(side, source, target).start()

    def finish_rest(self):
        for side, source, target, held, _ in self.ways(self.size - 1):
            @pl.when(held)
            def _():
                self.rest_copy(side, source, target).wait_recv()

        for side, source, target, _, onward in self.ways(self.size - 2):
            @pl.when(onward)
            def _():
                self.rest_copy(side, source, target).wait_send()

    def finish(self):
        for hop in range(self.size - 1):
            for side, source, target, _, onward in self.ways(hop):
                @pl.when(onward)
                def _():
                    self.copy(hop, side, source, target).wait_send()


def heads_kernel(
    nd, nm, clean_ref, noise_ref, embed_ref, position_ref, gain_ref, qgain_ref, kgain_ref,
    qkv_ref, out_weight_ref, held_ref, columns_ref, copies_ref,
    raised, pixels, blocks, embedded, means, squares, normed, weights, projected, outgoing,
    z_send, z_recv, w_send, w_recv, w_half, h_send, h_recv, g_send, g_recv, g_half,
    o_send, o_recv, r_send, r_recv, c_send, c_recv, load_sem, own_sem,
):
    me = lax.axis_index("dp")
    here = lax.axis_index("mp")
    patches = position_ref.shape[0]
    width = embed_ref.shape[1]
    count, rows_full = clean_ref.shape[0], blocks.shape[1]
    rows = round_up(count, 16)
    tail = count // 16 * 16
    total = nm * patches
    features = nd * width
    pairs, chunk = outgoing.shape[0], outgoing.shape[3]
    heads = chunk // HEAD_DIM

    def load(kind, pair):
        return pltpu.make_async_copy(
            qkv_ref.at[kind, :, pl.ds(pair * chunk, chunk)], weights.at[kind], load_sem.at[kind]
        )

    for kind in range(3):
        load(kind, 0).start()
    own_columns = out_weight_ref.at[:, pl.ds(pl.multiple_of(me * width, HEAD_DIM), width)]
    keep = [pltpu.make_async_copy(own_columns, columns_ref.at[here], own_sem.at[0])]
    keep[0].start()
    raised[...] = jnp.zeros_like(raised)
    raised[:count, :] = clean_ref[...].astype(jnp.float32) + 0.5 * noise_ref[...].astype(jnp.float32)
    pixels[here] = raised[...].T.astype(pixels.dtype)
    if rows_full > tail:
        blocks[:, tail:, :] = jnp.zeros((nd, rows_full - tail, width), blocks.dtype)
    blocks[me, :count, :] = embed_ref[...]
    greet((("dp", nd), ("mp", nm)))

    def pixel_copy(step):
        target = lax.rem(here + step, nm)
        return remote(
            pixels.at[here], pixels.at[here], z_send.at[step - 1], z_recv.at[here], "mp", target
        )

    for step in range(1, nm):
        pixel_copy(step).start()
    gather = Gather(
        nd,
        blocks.at[me, pl.ds(0, rows)],
        lambda s: blocks.at[s, pl.ds(0, rows)],
        lambda s, half: blocks.at[s, pl.ds(0, rows), pl.ds(half * (width // 2), width // 2)],
        w_send, w_recv, w_half,
    )
    gather.start()
    part = panel_width(width)
    apart = late_panel(nm) and width // part > 2
    early = pl.ds(0, width - (2 if apart else 1) * part)
    line = Line(nm, own_columns, lambda s: columns_ref.at[s], early, o_send, o_recv)
    line.second = pl.ds(width - 2 * part, part)
    line.rest_send, line.rest_recv = r_send, r_recv
    line.hop(0)
    for step in range(1, nm):
        source = lax.rem(here + step, nm)
        remote(
            pixels.at[here], pixels.at[source], z_send.at[0], z_recv.at[source], "mp", source
        ).wait_recv()

    band = 64

    done = []

    def embed(source):
        before = len(done)
        done.append(source)

        @pl.loop(0, width // part)
        def _(n):
            cols = pl.ds(pl.multiple_of(n * part, part), part)
            product = jnp.dot(
                pixels[...].reshape(total, rows_full),
                blocks[source, :, cols],
                preferred_element_type=jnp.float32,
            )
            place = position_ref[:, pl.ds(pl.multiple_of(source * width + n * part, part), part)]
            product = product.reshape(nm, patches, part) + place.astype(jnp.float32)[None]
            embedded[source, :, cols] = product.reshape(total, part)

        @pl.loop(0, total // band)
        def _(r):
            at = pl.ds(pl.multiple_of(r * band, band), band)
            values = embedded[source, at, :]
            mean = jnp.mean(values, axis=-1, keepdims=True)
            centred = values - mean
            square = jnp.sum(centred * centred, axis=-1, keepdims=True)
            if before == 0:
                means[at, :] = mean
                squares[at, :] = square
            else:
                apart = mean - means[at, :]
                means[at, :] += apart * (1.0 / (before + 1))
                squares[at, :] += square + apart * apart * (width * before / (before + 1))

    embed(me)
    steps = len(gather.order)
    gather.wait_slot(gather.sibling)
    embed(gather.sibling)
    if gather.relay:
        near = [gather.arrive(0), gather.arrive(1)]
        for source in near:
            embed(source)
        for step in range(2):
            embed(gather.arrive_sibling(step))
        far = gather.arrive(2)
        embed(far)
        line.hop(1)
        embed(gather.arrive_sibling(2))
    else:
        for step in range(steps):
            embed(gather.arrive(step))
        if nm > 1:
            line.hop(1)
        for step in range(steps):
            embed(gather.arrive_sibling(step))

    def copy_pixels(step):
        return remote(
            pixels.at[here], copies_ref.at[me], c_send.at[step - 1], c_recv.at[me], "dp",
            lax.rem(me + step, nd),
        )

    for step in range(1, nd):
        copy_pixels(step).start()
    keep.append(pltpu.make_async_copy(pixels.at[here], copies_ref.at[me], own_sem.at[1]))
    keep[1].start()

    @pl.loop(0, total // band)
    def _(r):
        at = pl.ds(pl.multiple_of(r * band, band), band)
        mean = means[at, :]
        scale = lax.rsqrt(squares[at, :] * (1.0 / features) + EPSILON)
        for s in range(nd):
            normed[at, s * width : (s + 1) * width] = (
                (embedded[s, at, :] - mean) * scale * gain_ref[s]
            ).astype(normed.dtype)

    def head_norm(values, gain):
        mean = jnp.mean(values, axis=-1, keepdims=True)
        centred = values - mean
        variance = jnp.mean(centred * centred, axis=-1, keepdims=True)
        return (centred * lax.rsqrt(variance + EPSILON) * gain[...]).astype(jnp.bfloat16)

    def exchange(pair, step):
        target = lax.rem(here + step, nm)
        return remote(
            outgoing.at[pair, target], held_ref.at[me, pair, here],
            h_send.at[pair, step - 1], h_recv.at[pair, here], "mp", target,
        )

    def keep_heads(pair):
        return pltpu.make_async_copy(
            outgoing.at[pair, here], held_ref.at[me, pair, here], own_sem.at[2 + pair]
        )

    shares = []

    def share(pair):
        keep_heads(pair).wait()
        for step in range(1, nm):
            source = lax.rem(here + step, nm)
            remote(
                outgoing.at[pair, source], held_ref.at[me, pair, source],
                h_send.at[pair, step - 1], h_recv.at[pair, source], "mp", source,
            ).wait_recv()
        shares.append(
            Gather(
                nd,
                held_ref.at[me, pair],
                lambda s: held_ref.at[s, pair],
                lambda s, half: held_ref.at[s, pair, pl.ds(half * (nm // 2), nm // 2)],
                g_send.at[pair], g_recv.at[pair], g_half.at[pair],
            )
        )
        shares[pair].start()

    def pass_near(pair):
        for step in range(min(2, steps)):
            shares[pair].arrive(step)

    def pass_far(pair):
        for step in range(2, steps):
            shares[pair].arrive(step)

    for pair in range(pairs):
        for kind in range(3):
            load(kind, pair).wait()
            projected[kind] = jnp.dot(
                normed[...], weights[kind], preferred_element_type=jnp.float32
            )
            if pair + 1 < pairs:
                load(kind, pair + 1).start()
            if kind == 1:
                if pair == min(1, pairs - 1):
                    for hop in range(2, min(3, nm)):
                        line.hop(hop)
                if pair >= 2:
                    pass_far(pair - 2)
                if pair >= 1:
                    share(pair - 1)

        for image in range(nm):
            at = slice(image * patches, (image + 1) * patches)
            for head in range(heads):
                cols = slice(head * HEAD_DIM, (head + 1) * HEAD_DIM)
                query = head_norm(projected[0, at, cols], qgain_ref)
                key = head_norm(projected[1, at, cols], kgain_ref)
                value = projected[2, at, cols].astype(jnp.bfloat16)
                scores = lax.dot_general(
                    query, key, (((1,), (1,)), ((), ())), preferred_element_type=jnp.float32
                ) * HEAD_DIM ** (-0.5)
                powers = jnp.exp(scores)
                probs = (powers / jnp.sum(powers, axis=-1, keepdims=True)).astype(jnp.bfloat16)
                result = jnp.dot(probs, value, preferred_element_type=jnp.float32)
                outgoing[pair, image, :, cols] = result.astype(jnp.bfloat16)

        for step in range(1, nm):
            exchange(pair, step).start()
        keep_heads(pair).start()
        if pair >= 1:
            pass_near(pair - 1)

    last = pairs - 1
    share(last)
    if apart and nm <= 4:
        line.rest()
    if last >= 1:
        pass_far(last - 1)
    pass_near(last)
    pass_far(last)

    for copy in keep:
        copy.wait()
    for hop in range(3, nm + 1):
        line.hop(hop)
    if apart:
        if nm > 4:
            line.rest()
        line.finish_rest()
    line.finish()
    for step in range(1, nm):
        pixel_copy(step).wait_send()
    for step in range(1, nd):
        copy_pixels(step).wait_send()
        source = lax.rem(me + step, nd)
        remote(
            pixels.at[here], copies_ref.at[source], c_send.at[0], c_recv.at[source], "dp", source
        ).wait_recv()
    gather.finish()
    for pair in range(pairs):
        for step in range(1, nm):
            exchange(pair, step).wait_send()
        for step in range(steps):
            shares[pair].arrive_sibling(step)
        shares[pair].wait_slot(shares[pair].sibling)
        shares[pair].finish()


def output_kernel(
    nd, nm, heads_ref, noisy_ref, embed_ref, position_ref, columns_ref, features_ref, smoothed_ref,
    weights, embed_full, outgoing, incoming, f_send, f_recv, late_send, late_recv, load_sem,
):
    me = lax.axis_index("dp")
    here = lax.axis_index("mp")
    _, pairs, _, patches, chunk = heads_ref.shape
    width = embed_ref.shape[1]
    count, rows_full = embed_ref.shape[0], noisy_ref.shape[2]
    group = columns_ref.shape[1]
    part = panel_width(width)
    panels = width // part
    early, late = pl.ds(0, width - part), pl.ds(width - part, part)
    both = 2 * patches

    first_load = pltpu.make_async_copy(
        columns_ref.at[:, :, early], weights.at[:, :, early], load_sem.at[nm]
    )
    first_load.start()

    def late_loads():
        for source in range(nm):
            near = (here - source < nm - 1) & (source - here < nm - 1)
            copy = pltpu.make_async_copy(
                columns_ref.at[source, :, late], weights.at[source, :, late], load_sem.at[source]
            )
            yield near if late_panel(nm) else here >= 0, copy

    for near, copy in late_loads():
        @pl.when(near)
        def _():
            copy.start()

    greet((("dp", nd), ("mp", nm)))

    def late_hop(side, step, source, target):
        return remote(
            columns_ref.at[source, :, late], weights.at[source, :, late],
            late_send.at[side], late_recv.at[side], "mp", target,
        )

    def late_sends():
        for side, step in enumerate((1, -1)):
            source, target = here - step * (nm - 2), here + step
            go = (source >= 0) & (source < nm) & (target >= 0) & (target < nm)
            yield go, late_hop(side, step, source, target)

    if late_panel(nm):
        for go, copy in late_sends():
            @pl.when(go)
            def _():
                copy.start()

    embed_full[count // 16 * 16 :, :] = jnp.zeros(
        (rows_full - count // 16 * 16, width), embed_full.dtype
    )
    embed_full[:count, :] = embed_ref[...]
    smoothed_ref[...] = jnp.zeros_like(smoothed_ref)

    def give(panel, copy):
        return remote(
            outgoing.at[panel, copy], incoming.at[panel, me],
            f_send.at[panel, copy], f_recv.at[panel, me], "dp", copy,
        )

    def project(panel, chip):
        pair = pl.ds(chip * 2, 2)
        cols = slice(panel * part, (panel + 1) * part)
        left = jnp.concatenate(
            [heads_ref[pair, p, h].reshape(both, chunk) for h in range(nm) for p in range(pairs)],
            axis=1,
        )
        product = jnp.dot(
            left, weights[:, :, cols].reshape(nm * group, part), preferred_element_type=jnp.float32
        )
        base = jnp.dot(
            noisy_ref[pair].reshape(both, rows_full), embed_full[:, cols],
            preferred_element_type=jnp.float32,
        )
        place = position_ref[:, pl.ds(pl.multiple_of(me * width + panel * part, part), part)]
        result = (product + base).reshape(2, patches, part) + place.astype(jnp.float32)[None]
        outgoing[panel, pair] = result.astype(outgoing.dtype)
        smoothed_ref[:, cols] += jnp.sum(result, axis=0) * (1.0 / nd)

    chip_here = me // 2
    chips = nd // 2
    sibling = chip_here * 2 + 1 - lax.rem(me, 2)
    first_load.wait()
    for panel in range(panels):
        if panel == panels - 1:
            for near, copy in late_loads():
                @pl.when(near)
                def _():
                    copy.wait()

            if late_panel(nm):
                for side, step in enumerate((1, -1)):
                    source = here - step * (nm - 1)

                    @pl.when((source >= 0) & (source < nm))
                    def _():
                        late_hop(side, step, source, here - step).wait_recv()

        for step in range(1, chips):
            chip = lax.rem(chip_here + step, chips)
            project(panel, chip)
            for core in range(2):
                give(panel, chip * 2 + core).start()
        project(panel, chip_here)
        give(panel, sibling).start()
        at = pl.ds(pl.multiple_of(me * width + panel * part, part), part)
        features_ref[:, at] = outgoing[panel, me]

    if late_panel(nm):
        for go, copy in late_sends():
            @pl.when(go)
            def _():
                copy.wait_send()

    for panel in range(panels):
        for step in range(1, nd):
            source = lax.rem(me + step, nd)
            give(panel, source).wait_send()
            remote(
                outgoing.at[panel, source], incoming.at[panel, source],
                f_send.at[panel, source], f_recv.at[panel, source], "dp", source,
            ).wait_recv()
            at = pl.ds(pl.multiple_of(source * width + panel * part, part), part)
            features_ref[:, at] = incoming[panel, source]


VMEM = pl.BlockSpec(memory_space=pltpu.VMEM)
DMA = pltpu.SemaphoreType.DMA


def on_device(
    clean_image, noise_draw, embed_weight, position_table, norm_gain, qkv_weight,
    query_gain, key_gain, out_weight,
):
    nd, nm = lax.axis_size("dp"), lax.axis_size("mp")
    patches, features = position_table.shape
    pixels, width = embed_weight.shape
    group = qkv_weight.shape[2]
    heads = group // HEAD_DIM
    chunk = HEAD_DIM * (2 if heads % 2 == 0 else 1)
    pairs = group // chunk
    rows_full = round_up(pixels, 128)

    part = panel_width(width)

    bf16, f32 = jnp.bfloat16, jnp.float32
    total = nm * patches
    anywhere = pl.BlockSpec(memory_space=pl.ANY)
    held, columns, copies = pl.pallas_call(
        functools.partial(heads_kernel, nd, nm),
        out_shape=(
            jax.ShapeDtypeStruct((nd, pairs, nm, patches, chunk), bf16),
            jax.ShapeDtypeStruct((nm, group, width), bf16),
            jax.ShapeDtypeStruct((nd, patches, rows_full), bf16),
        ),
        in_specs=[VMEM] * 7 + [anywhere] * 2,
        out_specs=(anywhere,) * 3,
        scratch_shapes=[
            pltpu.VMEM((rows_full, patches), f32),
            pltpu.VMEM((nm, patches, rows_full), bf16),
            pltpu.VMEM((nd, rows_full, width), bf16),
            pltpu.VMEM((nd, total, width), f32),
            pltpu.VMEM((total, 1), f32),
            pltpu.VMEM((total, 1), f32),
            pltpu.VMEM((total, features), bf16),
            pltpu.VMEM((3, features, chunk), bf16),
            pltpu.VMEM((3, total, chunk), f32),
            pltpu.VMEM((pairs, nm, patches, chunk), bf16),
            DMA((nm,)), DMA((nm,)),
            DMA((sends(nd),)), DMA((nd,)), DMA((2,)),
            DMA((pairs, nm)), DMA((pairs, nm)),
            DMA((pairs, sends(nd))), DMA((pairs, nd)), DMA((pairs, 2)),
            DMA((nm, 2)), DMA((nm,)), DMA((2,)), DMA((2,)),
            DMA((nd,)), DMA((nd,)),
            DMA((3,)), DMA((2 + pairs,)),
        ],
        compiler_params=pltpu.CompilerParams(
            collective_id=0, has_side_effects=True, vmem_limit_bytes=62 * 1024 * 1024
        ),
        cost_estimate=pl.CostEstimate(
            flops=2 * total * features * 4 * group, bytes_accessed=qkv_weight.size * 2,
            transcendentals=0,
        ),
        name="embed_and_heads",
    )(
        clean_image[0],
        noise_draw[0, 0],
        embed_weight,
        position_table,
        norm_gain.reshape(nd, 1, width),
        query_gain.reshape(1, HEAD_DIM),
        key_gain.reshape(1, HEAD_DIM),
        jnp.transpose(qkv_weight, (1, 0, 2)),
        out_weight,
    )

    features_out, smoothed = pl.pallas_call(
        functools.partial(output_kernel, nd, nm),
        out_shape=(
            jax.ShapeDtypeStruct((patches, features), bf16),
            jax.ShapeDtypeStruct((patches, width), f32),
        ),
        in_specs=[VMEM] * 4 + [anywhere],
        out_specs=(VMEM, VMEM),
        scratch_shapes=[
            pltpu.VMEM((nm, group, width), bf16),
            pltpu.VMEM((rows_full, width), bf16),
            pltpu.VMEM((width // part, nd, patches, part), bf16),
            pltpu.VMEM((width // part, nd, patches, part), bf16),
            DMA((width // part, nd)), DMA((width // part, nd)),
            DMA((2,)), DMA((2,)), DMA((nm + 1,)),
        ],
        compiler_params=pltpu.CompilerParams(
            collective_id=1, has_side_effects=True, vmem_limit_bytes=48 * 1024 * 1024
        ),
        cost_estimate=pl.CostEstimate(
            flops=2 * nd * patches * nm * group * width, bytes_accessed=2 * nm * group * width,
            transcendentals=0,
        ),
        name="project_and_share",
    )(held, copies, embed_weight, position_table, columns)
    return features_out[:, None, None, :], smoothed[:, None, :]


def solution(mesh):
    placed = (
        P("mp", None, None),
        P("mp", "dp", None, None),
        P(None, "dp"),
        P(),
        P(),
        P(None, None, "mp"),
        P(),
        P(),
        P("mp", None),
    )
    return jax.shard_map(
        on_device,
        mesh=mesh,
        in_specs=placed,
        out_specs=(P(None, "dp", "mp", None), P(None, "mp", "dp")),
        check_vma=False,
    )
```
